32 devices in a mesh: wide: 8 (over y, x, core), narrow: 4 (over z).
Axes of the slice: x: 2, y: 2, z: 4, core: 2. Of those that a mesh axis runs over, the one named last changes fastest.
Arguments:
- volume: bfloat16 [64, 16, 32, 512], P(None, 'wide', 'narrow'), may hold values from -6 to 6
- out_grad: bfloat16 [64, 16, 32, 512], P(None, 'wide', 'narrow'), may hold values from -6 to 6
- plane_kernel: bfloat16 [9, 64, 64], replicated, may hold values from -0.25 to 0.25
- z_axis_kernel: bfloat16 [7, 64, 64], replicated, may hold values from -0.25 to 0.25
Outputs:
- volume_grad: bfloat16 [64, 16, 32, 512], P(None, 'wide', 'narrow')
- plane_kernel_grad: float32 [9, 64, 64], replicated
- z_axis_kernel_gradient: float32 [7, 64, 64], replicated
The draws below stay inside these ranges and needn't reach their ends.
All inputs are finite; a program needn't handle non-finite values.
Results may differ from the reference program's by a relative error of at most 0.0061.
Values may be sent and summed in bfloat16 or wider, within the bound.
A program may use at most 192 MiB of HBM per device.

```python
import math
import jax
import jax.numpy as jnp

CH = 64
YB = 512
Z_DILATION = 4
NZ = 16
NX = 32


def block_scale(key, shape, shards, low, high):
    level, own = 1.0, jax.random.fold_in(key, 6)
    for position, shards_of in shards:
        heights = jnp.exp(jax.random.uniform(jax.random.fold_in(own, position), (shards_of,), jnp.float32, low / len(shards), high / len(shards)))
        level = level * jnp.repeat(heights, shape[position] // shards_of).reshape([-1 if axis == position else 1 for axis in range(len(shape))])
    return level


def gaussian(key, shape, scale, limit, split=(), kind=jnp.bfloat16):
    loudness = block_scale(key, shape, split, -0.22, 0.18) if split else 1.0
    array = jax.random.normal(key, shape, jnp.float32) * scale * loudness
    return jnp.minimum(jnp.maximum(array, -limit), limit).astype(kind)


def setup_inputs(seed: int = 0) -> dict:
    key_of = jax.random.split(jax.random.key(seed), 5)
    return {
        "volume": gaussian(key_of[0], (CH, NZ, NX, YB), 1.0, 6.0, ((1, 8), (2, 4))),
        "out_grad": gaussian(key_of[1], (CH, NZ, NX, YB), 1.0, 6.0, ((1, 8), (2, 4))),
        "plane_kernel": gaussian(key_of[2], (9, CH, CH), (9 * CH) ** -0.5, 0.25),
        "z_axis_kernel": gaussian(key_of[3], (7, CH, CH), (7 * CH) ** -0.5, 0.25),
    }


def silu_slope(values):
    sigmoid = jax.nn.sigmoid(values)
    return sigmoid * (1.0 + values * (1.0 - sigmoid))

def channel_mixing(weight, source):
    width = source.shape[0]
    mixed = jnp.dot(weight, source.reshape(width, -1), preferred_element_type=jnp.float32)
    return mixed.reshape((weight.shape[0],) + source.shape[1:])

def kernel_product(left, right):
    return jnp.dot(left.reshape(left.shape[0], -1), right.reshape(right.shape[0], -1).T, preferred_element_type=jnp.float32)

def plane_slice(padded, kernel_tap_index, rows, cols):
    row_shift = kernel_tap_index // 3
    col_shift = kernel_tap_index % 3
    return padded[:, :, row_shift:row_shift + rows, col_shift:col_shift + cols]

def depth_window(padded, start, depth_axis_size):
    return padded[:, start:start + depth_axis_size]

def reference(volume, out_grad, plane_kernel, z_axis_kernel):
    depth_axis_size = volume.shape[1]
    rows = volume.shape[2]
    cols = volume.shape[3]
    kernel_extent = 3 * Z_DILATION
    padded = jnp.pad(volume, ((0, 0), (0, 0), (1, 1), (1, 1)))
    pre_act = jnp.zeros(volume.shape, jnp.float32)
    for kernel_tap_index in range(9):
        pre_act = pre_act + channel_mixing(plane_kernel[kernel_tap_index], plane_slice(padded, kernel_tap_index, rows, cols))
    acts = jax.nn.silu(pre_act).astype(jnp.bfloat16)
    activation_padded = jnp.pad(acts, ((0, 0), (kernel_extent, kernel_extent), (0, 0), (0, 0)))
    depth_output = jnp.zeros(volume.shape, jnp.float32)
    for kernel_tap_index in range(7):
        depth_output = depth_output + channel_mixing(z_axis_kernel[kernel_tap_index], depth_window(activation_padded, kernel_tap_index * Z_DILATION, depth_axis_size))
    depth_gradient = (out_grad.astype(jnp.float32) * silu_slope(depth_output)).astype(jnp.bfloat16)
    gradient_scale = 1.0 / math.sqrt(depth_axis_size * rows * cols)
    z_axis_kernel_gradient = jnp.stack([kernel_product(depth_gradient, depth_window(activation_padded, kernel_tap_index * Z_DILATION, depth_axis_size)) for kernel_tap_index in range(7)]) * gradient_scale
    gradient_padded = jnp.pad(depth_gradient, ((0, 0), (kernel_extent, kernel_extent), (0, 0), (0, 0)))
    activation_gradient = jnp.zeros(volume.shape, jnp.float32)
    for kernel_tap_index in range(7):
        activation_gradient = activation_gradient + channel_mixing(z_axis_kernel[kernel_tap_index].T, depth_window(gradient_padded, (6 - kernel_tap_index) * Z_DILATION, depth_axis_size))
    activation_gradient = activation_gradient.astype(jnp.bfloat16)
    pre_grad = (activation_gradient.astype(jnp.float32) * silu_slope(pre_act)).astype(jnp.bfloat16)
    plane_kernel_grad = jnp.stack([kernel_product(pre_grad, plane_slice(padded, kernel_tap_index, rows, cols)) for kernel_tap_index in range(9)]) * gradient_scale
    pre_pad = jnp.pad(pre_grad, ((0, 0), (0, 0), (1, 1), (1, 1)))
    volume_grad = out_grad.astype(jnp.float32)
    for kernel_tap_index in range(9):
        volume_grad = volume_grad + channel_mixing(plane_kernel[kernel_tap_index].T, plane_slice(pre_pad, 8 - kernel_tap_index, rows, cols))
    return (volume_grad.astype(jnp.bfloat16), plane_kernel_grad, z_axis_kernel_gradient)
```

```python
import functools
import math

import jax
import jax.numpy as jnp
from jax import lax
from jax.experimental import pallas as pl
from jax.experimental.pallas import tpu as pltpu
from jax.sharding import PartitionSpec as P

Z_DILATION = 4


def with_halo(block, sides, width):
    for axis, dim in sides:
        count = lax.axis_size(axis)
        forward = [(i, i + 1) for i in range(count - 1)]
        backward = [(target, source) for source, target in forward]
        low = lax.ppermute(
            lax.slice_in_dim(block, block.shape[dim] - width, None, axis=dim), axis, forward
        )
        high = lax.ppermute(lax.slice_in_dim(block, 0, width, axis=dim), axis, backward)
        block = jnp.concatenate([low, block, high], axis=dim)
    return block


def silu_slope(values):
    sigmoid = jax.nn.sigmoid(values)
    return sigmoid * (1.0 + values * (1.0 - sigmoid))


def plane_stack(rimmed, rows, cols, flipped):
    padded = jnp.pad(rimmed, ((0, 0), (0, 0), (0, 0), (1, 1)))
    pieces = []
    for kernel_tap_index in range(9):
        source_tap = 8 - kernel_tap_index if flipped else kernel_tap_index
        row_shift = source_tap // 3
        col_shift = source_tap % 3
        pieces.append(padded[:, :, row_shift : row_shift + rows, col_shift : col_shift + cols])
    return jnp.concatenate(pieces, axis=0)


def depth_stack(pencil, kernel_extent, flipped):
    depth_axis_size = pencil.shape[1]
    padded = jnp.pad(pencil, ((0, 0), (kernel_extent, kernel_extent), (0, 0)))
    pieces = []
    for kernel_tap_index in range(7):
        source_tap = 6 - kernel_tap_index if flipped else kernel_tap_index
        start = source_tap * Z_DILATION
        pieces.append(padded[:, start : start + depth_axis_size])
    return jnp.concatenate(pieces, axis=0)


def stacked_mixing(weight, stacked, out_shape):
    mixed = jnp.dot(
        weight, stacked.reshape(stacked.shape[0], -1), preferred_element_type=jnp.float32
    )
    return mixed.reshape(out_shape)


def stacked_kernel_grad(left, stacked, taps):
    width = left.shape[0]
    product = jnp.dot(
        left.reshape(width, -1),
        stacked.reshape(stacked.shape[0], -1).T,
        preferred_element_type=jnp.float32,
    )
    return product.reshape(width, taps, width).transpose(1, 0, 2)


def on_device(volume, out_grad, plane_kernel, z_axis_kernel):
    width, slabs, rows, cols = volume.shape
    cells = rows * cols
    kernel_extent = 3 * Z_DILATION
    plane_forward = plane_kernel.transpose(1, 0, 2).reshape(width, 9 * width)
    plane_backward = plane_kernel.transpose(2, 0, 1).reshape(width, 9 * width)
    depth_forward = z_axis_kernel.transpose(1, 0, 2).reshape(width, 7 * width)
    depth_backward = z_axis_kernel.transpose(2, 0, 1).reshape(width, 7 * width)
    rimmed = with_halo(volume, (("narrow", 2),), 1)
    volume_stack = plane_stack(rimmed, rows, cols, False)
    pre_act = stacked_mixing(plane_forward, volume_stack, volume.shape)
    acts = jax.nn.silu(pre_act).astype(jnp.bfloat16)
    act_slab = acts.reshape(width, slabs, cells)
    act_pencil, grad_pencil = (
        lax.all_to_all(act_slab, "wide", split_axis=2, concat_axis=1, tiled=True),
        lax.all_to_all(
            out_grad.reshape(width, slabs, cells), "wide", split_axis=2, concat_axis=1, tiled=True
        ),
    )
    depth_axis_size = act_pencil.shape[1]
    act_stack = depth_stack(act_pencil, kernel_extent, False)
    depth_output = stacked_mixing(depth_forward, act_stack, act_pencil.shape)
    depth_gradient = (grad_pencil.astype(jnp.float32) * silu_slope(depth_output)).astype(
        jnp.bfloat16
    )
    depth_term = stacked_kernel_grad(depth_gradient, act_stack, 7)
    grad_stack = depth_stack(depth_gradient, kernel_extent, True)
    activation_gradient = stacked_mixing(depth_backward, grad_stack, act_pencil.shape).astype(
        jnp.bfloat16
    )
    slab_grad = lax.all_to_all(
        activation_gradient, "wide", split_axis=1, concat_axis=2, tiled=True
    ).reshape(width, slabs, rows, cols)
    gradient_scale = 1.0 / math.sqrt(depth_axis_size * rows * lax.axis_size("narrow") * cols)
    pre_grad = (slab_grad.astype(jnp.float32) * silu_slope(pre_act)).astype(jnp.bfloat16)
    plane_term = stacked_kernel_grad(pre_grad, volume_stack, 9)
    grad_rimmed = with_halo(pre_grad, (("narrow", 2),), 1)
    pre_stack = plane_stack(grad_rimmed, rows, cols, True)
    volume_grad = out_grad.astype(jnp.float32) + stacked_mixing(
        plane_backward, pre_stack, volume.shape
    )
    plane_total, depth_total = lax.psum((plane_term, depth_term), ("wide", "narrow"))
    return (
        volume_grad.astype(jnp.bfloat16),
        plane_total * gradient_scale,
        depth_total * gradient_scale,
    )


BF16 = jnp.bfloat16
F32 = jnp.float32
MESH = pl.DeviceIdType.MESH
TILES = 12


def sigmoid_of(values):
    return 0.5 * jnp.tanh(0.5 * values) + 0.5


def shifted_stack(row):
    wide_row = row.astype(F32)
    cols = row.shape[1]
    column = lax.broadcasted_iota(jnp.int32, row.shape, 1)
    left = jnp.where(column == 0, 0.0, pltpu.roll(wide_row, 1, 1))
    right = jnp.where(column == cols - 1, 0.0, pltpu.roll(wide_row, cols - 1, 1))
    return jnp.concatenate([left.astype(BF16), row.astype(BF16), right.astype(BF16)], axis=0)


def dot_nn(left, right):
    return jnp.dot(left, right, preferred_element_type=F32)


def dot_nt(left, right):
    return lax.dot_general(left, right, (((1,), (1,)), ((), ())), preferred_element_type=F32)


def block_kernel(
    n, m, rows, scale,
    vol, og, wf, wb, bigw, bigw_t,
    vg, gsum,
    volh, stack, slope, acts_out, acts_in, og_in, dg, ag_out, ag_in, pg_halo, plane_acc, depth_acc,
    red_src, red_in, part, part_in, tot, tot_in,
    vh_s, vh_r, og_s, og_r, ac_s, ac_r, ag_s, ag_r, ph_s, ph_r, r1_s, r1_r, r2_s, r2_r, r3_s, r3_r,
):
    me = lax.axis_index("wide")
    mine = lax.axis_index("narrow")
    ch = vol.shape[2]
    cols = vol.shape[3]

    def rcopy(source, target, send, recv, **where):
        return pltpu.make_async_remote_copy(
            src_ref=source, dst_ref=target, send_sem=send, recv_sem=recv,
            device_id=where, device_id_type=MESH,
        )

    def wide_peer(step):
        return lax.rem(me + step, n)

    def narrow_peer(step):
        return lax.rem(mine + step, m)

    barrier = pltpu.get_barrier_semaphore()

    @pl.loop(1, n)
    def _(step):
        pl.semaphore_signal(barrier, inc=1, device_id={"wide": wide_peer(step)}, device_id_type=MESH)

    @pl.loop(1, m)
    def _(step):
        pl.semaphore_signal(barrier, inc=1, device_id={"narrow": narrow_peer(step)}, device_id_type=MESH)

    pl.semaphore_wait(barrier, n + m - 2)

    has_low = mine > 0
    has_high = mine < m - 1
    up = jnp.minimum(mine + 1, m - 1)
    down = jnp.maximum(mine - 1, 0)

    def vol_up():
        return rcopy(vol.at[rows - 1], volh.at[0], vh_s.at[0], vh_r.at[0], narrow=up)

    def vol_down():
        return rcopy(vol.at[0], volh.at[rows + 1], vh_s.at[1], vh_r.at[1], narrow=down)

    def og_copy(step):
        peer = wide_peer(step)
        return rcopy(og.at[peer], og_in.at[me // 2, lax.rem(me, 2)], og_s.at[peer], og_r.at[me], wide=peer)

    def og_arrival(step):
        peer = wide_peer(step)
        return rcopy(og.at[peer], og_in.at[peer // 2, lax.rem(peer, 2)], og_s.at[peer], og_r.at[peer], wide=peer)

    def act_copy(peer):
        return rcopy(acts_out.at[peer], acts_in.at[me // 2, lax.rem(me, 2)], ac_s.at[peer], ac_r.at[me], wide=peer)

    def act_arrival(peer):
        return rcopy(acts_out.at[peer], acts_in.at[peer // 2, lax.rem(peer, 2)], ac_s.at[peer], ac_r.at[peer], wide=peer)

    def ag_copy(peer):
        return rcopy(ag_out.at[peer // 2, lax.rem(peer, 2)], ag_in.at[me], ag_s.at[peer], ag_r.at[me], wide=peer)

    def ag_arrival(peer):
        return rcopy(ag_out.at[peer // 2, lax.rem(peer, 2)], ag_in.at[peer], ag_s.at[peer], ag_r.at[peer], wide=peer)

    def pg_up():
        return rcopy(stack.at[rows, :, pl.ds(ch, ch)], pg_halo.at[0], ph_s.at[0], ph_r.at[0], narrow=up)

    def pg_down():
        return rcopy(stack.at[1, :, pl.ds(ch, ch)], pg_halo.at[1], ph_s.at[1], ph_r.at[1], narrow=down)

    def r1_copy(peer):
        return rcopy(red_src.at[peer], red_in.at[me], r1_s.at[peer], r1_r.at[me], wide=peer)

    def r1_arrival(peer):
        return rcopy(red_src.at[peer], red_in.at[peer], r1_s.at[peer], r1_r.at[peer], wide=peer)

    def r2_copy(peer):
        return rcopy(part, part_in.at[mine], r2_s.at[peer], r2_r.at[mine], narrow=peer)

    def r2_arrival(peer):
        return rcopy(part, part_in.at[peer], r2_s.at[peer], r2_r.at[peer], narrow=peer)

    def r3_copy(peer):
        return rcopy(tot, tot_in.at[me], r3_s.at[peer], r3_r.at[me], wide=peer)

    def r3_arrival(peer):
        return rcopy(tot, tot_in.at[peer], r3_s.at[peer], r3_r.at[peer], wide=peer)

    @pl.when(has_high)
    def _():
        vol_up().start()

    @pl.when(has_low)
    def _():
        vol_down().start()

    @pl.loop(1, n)
    def _(step):
        og_copy(step).start()

    og_in[me // 2, lax.rem(me, 2)] = og[me]

    @pl.when(jnp.logical_not(has_low))
    def _():
        volh[0] = jnp.zeros(volh.shape[1:], BF16)

    @pl.when(jnp.logical_not(has_high))
    def _():
        volh[rows + 1] = jnp.zeros(volh.shape[1:], BF16)

    @pl.loop(0, rows)
    def _(x):
        for z in range(2):
            row = vol[x, z]
            volh[x + 1, z] = row
            stack[x + 1, z] = shifted_stack(row)

    @pl.when(has_high)
    def _():
        vol_up().wait_send()
        vol_down().wait_recv()

    @pl.when(has_low)
    def _():
        vol_down().wait_send()
        vol_up().wait_recv()

    for x in (0, rows + 1):
        for z in range(2):
            stack[x, z] = shifted_stack(volh[x, z])

    @pl.loop(1, n + 1)
    def _(step):
        x = wide_peer(step)
        for z in range(2):
            v = dot_nn(wf[...], stack[pl.ds(x, 3), z].reshape(9 * ch, cols))
            g = sigmoid_of(v)
            acts_out[x, z] = (v * g).astype(BF16)
            slope[x, z] = g * (1.0 + v * (1.0 - g))

        @pl.when(step < n)
        def _():
            act_copy(x).start()

    acts_in[me // 2, lax.rem(me, 2)] = acts_out[me]

    @pl.loop(1, n)
    def _(step):
        og_arrival(step).wait_recv()
        act_arrival(wide_peer(step)).wait_recv()

    @pl.loop(0, 2)
    def _(half):
        for b in range(2):
            pencil = acts_in[:, half, b].reshape(4 * ch, cols)
            v = dot_nn(bigw[...], pencil)
            g = sigmoid_of(v)
            cot = og_in[:, half, b].reshape(4 * ch, cols).astype(F32)
            grad = (cot * (g * (1.0 + v * (1.0 - g)))).astype(BF16)
            dg[half, b] = grad
            back = dot_nn(bigw_t[...], grad).astype(BF16)
            ag_out[:, half, b] = back.reshape(4, ch, cols)
        for q in range(4):
            peer = 2 * q + half

            @pl.when(peer != me)
            def _():
                ag_copy(peer).start()

            @pl.when(peer == me)
            def _():
                ag_in[me] = ag_out[q, half]

    depth_acc[...] = jnp.zeros_like(depth_acc)
    plane_acc[...] = jnp.zeros_like(plane_acc)

    @pl.loop(0, 2)
    def _(half):
        for b in range(2):
            depth_acc[...] += dot_nt(dg[half, b], acts_in[:, half, b].reshape(4 * ch, cols))

    for d in range(-3, 3):
        tile = jnp.zeros((ch, 128), F32)
        for q in range(4):
            for t in range(2):
                if 2 * t - q == d:
                    tile = tile + depth_acc[q * ch : (q + 1) * ch, 128 * t : 128 * (t + 1)]
        red_src[:, d + 3] = tile.reshape(n, ch // n, 128)

    @pl.loop(0, rows)
    def _(step):
        x = lax.rem(step + rows - 1, rows)

        @pl.when(x != me)
        def _():
            ag_arrival(x).wait_recv()

        for z in range(2):
            row = ag_in[x, z].astype(F32) * slope[x, z]
            shifted = shifted_stack(row.astype(BF16))
            stack[x + 1, z] = shifted
            plane_acc[...] += dot_nt(shifted, volh[pl.ds(x, 3), z].reshape(3 * ch, cols))

        @pl.when(step == 1)
        def _():
            @pl.when(has_high)
            def _():
                pg_up().start()

            @pl.when(has_low)
            def _():
                pg_down().start()

    for s in range(3):
        red_src[:, 6 + 2 * s] = plane_acc[s * ch : (s + 1) * ch, 0:128].reshape(n, ch // n, 128)
        rest = jnp.concatenate(
            [plane_acc[s * ch : (s + 1) * ch, 128:192], jnp.zeros((ch, 64), F32)], axis=1
        )
        red_src[:, 7 + 2 * s] = rest.reshape(n, ch // n, 128)

    @pl.loop(1, n)
    def _(step):
        r1_copy(wide_peer(step)).start()

    red_in[me] = red_src[me]

    def volume_rows(low, high):
        @pl.loop(low, high)
        def _(x):
            for z in range(2):
                out = dot_nn(wb[...], stack[pl.ds(x, 3), z].reshape(9 * ch, cols))
                vg[x, z] = (og[x, z].astype(F32) + out).astype(BF16)

    volume_rows(1, 3)

    @pl.loop(1, n)
    def _(step):
        r1_arrival(wide_peer(step)).wait_recv()

    part[...] = jnp.sum(red_in[...], axis=0)

    @pl.loop(1, m)
    def _(step):
        r2_copy(narrow_peer(step)).start()

    part_in[mine] = part[...]
    volume_rows(3, 5)

    @pl.loop(1, m)
    def _(step):
        r2_arrival(narrow_peer(step)).wait_recv()

    tot[...] = jnp.sum(part_in[...], axis=0) * scale

    @pl.loop(1, n)
    def _(step):
        r3_copy(wide_peer(step)).start()

    tot_in[me] = tot[...]
    volume_rows(5, rows - 1)

    @pl.when(has_high)
    def _():
        pg_up().wait_send()
        pg_down().wait_recv()

    @pl.when(has_low)
    def _():
        pg_down().wait_send()
        pg_up().wait_recv()

    @pl.when(has_low)
    def _():
        for z in range(2):
            stack[0, z] = shifted_stack(pg_halo[0, z])

    @pl.when(has_high)
    def _():
        for z in range(2):
            stack[rows + 1, z] = shifted_stack(pg_halo[1, z])

    @pl.when(jnp.logical_not(has_low))
    def _():
        stack[0] = jnp.zeros(stack.shape[1:], BF16)

    @pl.when(jnp.logical_not(has_high))
    def _():
        stack[rows + 1] = jnp.zeros(stack.shape[1:], BF16)

    volume_rows(0, 1)
    volume_rows(rows - 1, rows)

    @pl.loop(1, n)
    def _(step):
        peer = wide_peer(step)
        r3_arrival(peer).wait_recv()
        og_copy(step).wait_send()
        act_copy(peer).wait_send()
        ag_copy(peer).wait_send()
        r1_copy(peer).wait_send()
        r3_copy(peer).wait_send()

    @pl.loop(1, m)
    def _(step):
        r2_copy(narrow_peer(step)).wait_send()

    gsum[...] = tot_in[...]


def fused_block(n, m, volume, out_grad, plane_kernel, z_axis_kernel):
    ch, _, rows, cols = volume.shape
    vol = volume.transpose(2, 1, 0, 3)
    og = out_grad.transpose(2, 1, 0, 3)
    wf = plane_kernel.transpose(1, 0, 2).reshape(ch, 9 * ch)
    wb = plane_kernel[::-1].transpose(2, 0, 1).reshape(ch, 9 * ch)
    bigw = jnp.concatenate(
        [z_axis_kernel[3 - q : 7 - q].transpose(1, 0, 2).reshape(ch, 4 * ch) for q in range(4)], axis=0
    )
    scale = 1.0 / math.sqrt(2 * n * rows * m * cols)
    own = (rows, 2, ch, cols)
    pencil = (4, 2, 2, ch, cols)
    piece = (TILES, ch // n, 128)
    sems = []
    for count in (2, n, n, n, 2, n, m, n):
        sems += [pltpu.SemaphoreType.DMA((count,))] * 2
    vmem = pl.BlockSpec(memory_space=pltpu.VMEM)
    vg, gsum = pl.pallas_call(
        functools.partial(block_kernel, n, m, rows, scale),
        out_shape=(jax.ShapeDtypeStruct(own, BF16), jax.ShapeDtypeStruct((n,) + piece, F32)),
        in_specs=[vmem] * 6,
        out_specs=(vmem, vmem),
        scratch_shapes=[
            pltpu.VMEM((rows + 2, 2, ch, cols), BF16),
            pltpu.VMEM((rows + 2, 2, 3 * ch, cols), BF16),
            pltpu.VMEM(own, F32),
            pltpu.VMEM(own, BF16),
            pltpu.VMEM(pencil, BF16),
            pltpu.VMEM(pencil, BF16),
            pltpu.VMEM((2, 2, 4 * ch, cols), BF16),
            pltpu.VMEM(pencil, BF16),
            pltpu.VMEM((n, 2, ch, cols), BF16),
            pltpu.VMEM((2, 2, ch, cols), BF16),
            pltpu.VMEM((3 * ch, 3 * ch), F32),
            pltpu.VMEM((4 * ch, 4 * ch), F32),
            pltpu.VMEM((n,) + piece, F32),
            pltpu.VMEM((n,) + piece, F32),
            pltpu.VMEM(piece, F32),
            pltpu.VMEM((m,) + piece, F32),
            pltpu.VMEM(piece, F32),
            pltpu.VMEM((n,) + piece, F32),
        ]
        + sems,
        compiler_params=pltpu.CompilerParams(
            collective_id=0, has_side_effects=True, vmem_limit_bytes=52 * 1024 * 1024
        ),
    )(vol, og, wf, wb, bigw, bigw.T)
    tiles = gsum.transpose(1, 0, 2, 3).reshape(TILES, ch, 2, ch)
    low = tiles[:6, :, 0]
    high = tiles[:6, :, 1]
    edge = jnp.zeros((1, ch, ch), F32)
    depth = jnp.concatenate([low, edge]) + jnp.concatenate([edge, high])
    plane = tiles[6:].reshape(3, 2, ch, 2, ch)[::-1].transpose(1, 3, 0, 2, 4)
    plane = plane.reshape(4, 3, ch, ch)[:3].reshape(9, ch, ch)
    return vg.transpose(2, 1, 0, 3), plane, depth


def solution(mesh):
    n, m = mesh.shape["wide"], mesh.shape["narrow"]

    def body(volume, out_grad, plane_kernel, z_axis_kernel):
        ch, slabs, rows, cols = volume.shape
        if n == 8 and slabs == 2 and rows == n and ch == 64 and m > 1:
            return fused_block(n, m, volume, out_grad, plane_kernel, z_axis_kernel)
        return on_device(volume, out_grad, plane_kernel, z_axis_kernel)

    return jax.shard_map(
        body,
        mesh=mesh,
        in_specs=(P(None, "wide", "narrow", None), P(None, "wide", "narrow", None), P(), P()),
        out_specs=(P(None, "wide", "narrow", None), P(), P()),
        check_vma=False,
    )
```

```python
import functools
import math

import jax
import jax.numpy as jnp
from jax import lax
from jax.experimental import pallas as pl
from jax.experimental.pallas import tpu as pltpu
from jax.sharding import PartitionSpec as P

Z_DILATION = 4


def with_halo(block, sides, width):
    for axis, dim in sides:
        count = lax.axis_size(axis)
        forward = [(i, i + 1) for i in range(count - 1)]
        backward = [(target, source) for source, target in forward]
        low = lax.ppermute(
            lax.slice_in_dim(block, block.shape[dim] - width, None, axis=dim), axis, forward
        )
        high = lax.ppermute(lax.slice_in_dim(block, 0, width, axis=dim), axis, backward)
        block = jnp.concatenate([low, block, high], axis=dim)
    return block


def silu_slope(values):
    sigmoid = jax.nn.sigmoid(values)
    return sigmoid * (1.0 + values * (1.0 - sigmoid))


def plane_stack(rimmed, rows, cols, flipped):
    padded = jnp.pad(rimmed, ((0, 0), (0, 0), (0, 0), (1, 1)))
    pieces = []
    for kernel_tap_index in range(9):
        source_tap = 8 - kernel_tap_index if flipped else kernel_tap_index
        row_shift = source_tap // 3
        col_shift = source_tap % 3
        pieces.append(padded[:, :, row_shift : row_shift + rows, col_shift : col_shift + cols])
    return jnp.concatenate(pieces, axis=0)


def depth_stack(pencil, kernel_extent, flipped):
    depth_axis_size = pencil.shape[1]
    padded = jnp.pad(pencil, ((0, 0), (kernel_extent, kernel_extent), (0, 0)))
    pieces = []
    for kernel_tap_index in range(7):
        source_tap = 6 - kernel_tap_index if flipped else kernel_tap_index
        start = source_tap * Z_DILATION
        pieces.append(padded[:, start : start + depth_axis_size])
    return jnp.concatenate(pieces, axis=0)


def stacked_mixing(weight, stacked, out_shape):
    mixed = jnp.dot(
        weight, stacked.reshape(stacked.shape[0], -1), preferred_element_type=jnp.float32
    )
    return mixed.reshape(out_shape)


def stacked_kernel_grad(left, stacked, taps):
    width = left.shape[0]
    product = jnp.dot(
        left.reshape(width, -1),
        stacked.reshape(stacked.shape[0], -1).T,
        preferred_element_type=jnp.float32,
    )
    return product.reshape(width, taps, width).transpose(1, 0, 2)


def on_device(volume, out_grad, plane_kernel, z_axis_kernel):
    width, slabs, rows, cols = volume.shape
    cells = rows * cols
    kernel_extent = 3 * Z_DILATION
    plane_forward = plane_kernel.transpose(1, 0, 2).reshape(width, 9 * width)
    plane_backward = plane_kernel.transpose(2, 0, 1).reshape(width, 9 * width)
    depth_forward = z_axis_kernel.transpose(1, 0, 2).reshape(width, 7 * width)
    depth_backward = z_axis_kernel.transpose(2, 0, 1).reshape(width, 7 * width)
    rimmed = with_halo(volume, (("narrow", 2),), 1)
    volume_stack = plane_stack(rimmed, rows, cols, False)
    pre_act = stacked_mixing(plane_forward, volume_stack, volume.shape)
    acts = jax.nn.silu(pre_act).astype(jnp.bfloat16)
    act_slab = acts.reshape(width, slabs, cells)
    act_pencil, grad_pencil = (
        lax.all_to_all(act_slab, "wide", split_axis=2, concat_axis=1, tiled=True),
        lax.all_to_all(
            out_grad.reshape(width, slabs, cells), "wide", split_axis=2, concat_axis=1, tiled=True
        ),
    )
    depth_axis_size = act_pencil.shape[1]
    act_stack = depth_stack(act_pencil, kernel_extent, False)
    depth_output = stacked_mixing(depth_forward, act_stack, act_pencil.shape)
    depth_gradient = (grad_pencil.astype(jnp.float32) * silu_slope(depth_output)).astype(
        jnp.bfloat16
    )
    depth_term = stacked_kernel_grad(depth_gradient, act_stack, 7)
    grad_stack = depth_stack(depth_gradient, kernel_extent, True)
    activation_gradient = stacked_mixing(depth_backward, grad_stack, act_pencil.shape).astype(
        jnp.bfloat16
    )
    slab_grad = lax.all_to_all(
        activation_gradient, "wide", split_axis=1, concat_axis=2, tiled=True
    ).reshape(width, slabs, rows, cols)
    gradient_scale = 1.0 / math.sqrt(depth_axis_size * rows * lax.axis_size("narrow") * cols)
    pre_grad = (slab_grad.astype(jnp.float32) * silu_slope(pre_act)).astype(jnp.bfloat16)
    plane_term = stacked_kernel_grad(pre_grad, volume_stack, 9)
    grad_rimmed = with_halo(pre_grad, (("narrow", 2),), 1)
    pre_stack = plane_stack(grad_rimmed, rows, cols, True)
    volume_grad = out_grad.astype(jnp.float32) + stacked_mixing(
        plane_backward, pre_stack, volume.shape
    )
    plane_total, depth_total = lax.psum((plane_term, depth_term), ("wide", "narrow"))
    return (
        volume_grad.astype(jnp.bfloat16),
        plane_total * gradient_scale,
        depth_total * gradient_scale,
    )


BF16 = jnp.bfloat16
F32 = jnp.float32
MESH = pl.DeviceIdType.MESH
DEPTH_ROWS = 32
PLANE_ROWS = 48
ALL_ROWS = 80


def sigmoid_of(values):
    return 0.5 * jnp.tanh(0.5 * values) + 0.5


def shifted_stack(row):
    wide_row = row.astype(F32)
    cols = row.shape[1]
    column = lax.broadcasted_iota(jnp.int32, row.shape, 1)
    left = jnp.where(column == 0, 0.0, pltpu.roll(wide_row, 1, 1))
    right = jnp.where(column == cols - 1, 0.0, pltpu.roll(wide_row, cols - 1, 1))
    return jnp.concatenate([left.astype(BF16), row.astype(BF16), right.astype(BF16)], axis=0)


def dot_nn(left, right):
    return jnp.dot(left, right, preferred_element_type=F32)


def dot_nt(left, right):
    return lax.dot_general(left, right, (((1,), (1,)), ((), ())), preferred_element_type=F32)


def block_kernel(
    n, m, rows, scale,
    vol, og, plane_w, depth_w,
    vg, plane_out, depth_out,
    wf, wb, bigw, bigw_t,
    volh, stack, slope, acts_out, acts_in, og_in, dg, ag_out, ag_in, pg_halo, plane_acc, depth_acc,
    red_f, zr_src, zr_in, red_src, red_in, part, part_in, tot, tot_in,
    vh_s, vh_r, og_s, og_r, ac_s, ac_r, ag_s, ag_r, ph_s, ph_r, z1_s, z1_r, r1_s, r1_r, r2_s, r2_r, r3_s, r3_r,
):
    me = lax.axis_index("wide")
    mine = lax.axis_index("narrow")
    ch = vol.shape[2]
    cols = vol.shape[3]

    def rcopy(source, target, send, recv, **where):
        return pltpu.make_async_remote_copy(
            src_ref=source, dst_ref=target, send_sem=send, recv_sem=recv,
            device_id=where, device_id_type=MESH,
        )

    def wide_peer(step):
        return lax.rem(me + step, n)

    def narrow_peer(step):
        return lax.rem(mine + step, m)

    barrier = pltpu.get_barrier_semaphore()

    @pl.loop(1, n)
    def _(step):
        pl.semaphore_signal(barrier, inc=1, device_id={"wide": wide_peer(step)}, device_id_type=MESH)

    @pl.loop(1, m)
    def _(step):
        pl.semaphore_signal(barrier, inc=1, device_id={"narrow": narrow_peer(step)}, device_id_type=MESH)

    for t in range(4):
        wf[:, 128 * t : 128 * (t + 1)] = jnp.concatenate([plane_w[2 * t], plane_w[2 * t + 1]], axis=1)
        pair = jnp.concatenate([plane_w[8 - 2 * t], plane_w[7 - 2 * t]], axis=0)
        wb[:, 128 * t : 128 * (t + 1)] = pair.astype(F32).T.astype(BF16)
    wf[:, 512:576] = plane_w[8]
    wb[:, 512:576] = plane_w[0].astype(F32).T.astype(BF16)
    for q in range(4):
        band = jnp.concatenate([depth_w[3 - q + p] for p in range(4)], axis=1)
        bigw[q * ch : (q + 1) * ch] = band
        bigw_t[:, q * ch : (q + 1) * ch] = band.astype(F32).T.astype(BF16)

    pl.semaphore_wait(barrier, n + m - 2)

    has_low = mine > 0
    has_high = mine < m - 1
    up = jnp.minimum(mine + 1, m - 1)
    down = jnp.maximum(mine - 1, 0)

    def vol_up():
        return rcopy(vol.at[rows - 1], volh.at[0], vh_s.at[0], vh_r.at[0], narrow=up)

    def vol_down():
        return rcopy(vol.at[0], volh.at[rows + 1], vh_s.at[1], vh_r.at[1], narrow=down)

    def og_copy(step):
        peer = wide_peer(step)
        return rcopy(og.at[peer], og_in.at[me // 2, lax.rem(me, 2)], og_s.at[peer], og_r.at[me], wide=peer)

    def og_arrival(step):
        peer = wide_peer(step)
        return rcopy(og.at[peer], og_in.at[peer // 2, lax.rem(peer, 2)], og_s.at[peer], og_r.at[peer], wide=peer)

    def act_copy(peer):
        return rcopy(acts_out.at[peer], acts_in.at[me // 2, lax.rem(me, 2)], ac_s.at[peer], ac_r.at[me], wide=peer)

    def act_arrival(peer):
        return rcopy(acts_out.at[peer], acts_in.at[peer // 2, lax.rem(peer, 2)], ac_s.at[peer], ac_r.at[peer], wide=peer)

    def ag_copy(peer):
        return rcopy(ag_out.at[peer // 2, lax.rem(peer, 2)], ag_in.at[me], ag_s.at[peer], ag_r.at[me], wide=peer)

    def ag_arrival(peer):
        return rcopy(ag_out.at[peer // 2, lax.rem(peer, 2)], ag_in.at[peer], ag_s.at[peer], ag_r.at[peer], wide=peer)

    def pg_up():
        return rcopy(stack.at[rows, :, pl.ds(ch, ch)], pg_halo.at[0], ph_s.at[0], ph_r.at[0], narrow=up)

    def pg_down():
        return rcopy(stack.at[1, :, pl.ds(ch, ch)], pg_halo.at[1], ph_s.at[1], ph_r.at[1], narrow=down)

    def z1_copy(peer):
        return rcopy(zr_src.at[peer], zr_in.at[me], z1_s.at[peer], z1_r.at[me], wide=peer)

    def z1_arrival(peer):
        return rcopy(zr_src.at[peer], zr_in.at[peer], z1_s.at[peer], z1_r.at[peer], wide=peer)

    def r1_copy(peer):
        return rcopy(red_src.at[peer], red_in.at[me], r1_s.at[peer], r1_r.at[me], wide=peer)

    def r1_arrival(peer):
        return rcopy(red_src.at[peer], red_in.at[peer], r1_s.at[peer], r1_r.at[peer], wide=peer)

    def r2_copy(peer):
        return rcopy(part, part_in.at[mine], r2_s.at[peer], r2_r.at[mine], narrow=peer)

    def r2_arrival(peer):
        return rcopy(part, part_in.at[peer], r2_s.at[peer], r2_r.at[peer], narrow=peer)

    def r3_copy(peer):
        return rcopy(tot, tot_in.at[me], r3_s.at[peer], r3_r.at[me], wide=peer)

    def r3_arrival(peer):
        return rcopy(tot, tot_in.at[peer], r3_s.at[peer], r3_r.at[peer], wide=peer)

    @pl.when(has_high)
    def _():
        vol_up().start()

    @pl.when(has_low)
    def _():
        vol_down().start()

    @pl.loop(1, n)
    def _(step):
        og_copy(step).start()

    og_in[me // 2, lax.rem(me, 2)] = og[me]

    @pl.when(jnp.logical_not(has_low))
    def _():
        volh[0] = jnp.zeros(volh.shape[1:], BF16)

    @pl.when(jnp.logical_not(has_high))
    def _():
        volh[rows + 1] = jnp.zeros(volh.shape[1:], BF16)

    @pl.loop(0, rows)
    def _(x):
        for z in range(2):
            row = vol[x, z]
            volh[x + 1, z] = row
            stack[x + 1, z] = shifted_stack(row)

    @pl.when(has_high)
    def _():
        vol_up().wait_send()
        vol_down().wait_recv()

    @pl.when(has_low)
    def _():
        vol_down().wait_send()
        vol_up().wait_recv()

    for x in (0, rows + 1):
        for z in range(2):
            stack[x, z] = shifted_stack(volh[x, z])

    @pl.loop(1, n + 1)
    def _(step):
        x = wide_peer(step)
        for z in range(2):
            v = dot_nn(wf[...], stack[pl.ds(x, 3), z].reshape(9 * ch, cols))
            g = sigmoid_of(v)
            acts_out[x, z] = (v * g).astype(BF16)
            slope[x, z] = g * (1.0 + v * (1.0 - g))

        @pl.when(step < n)
        def _():
            act_copy(x).start()

    acts_in[me // 2, lax.rem(me, 2)] = acts_out[me]

    @pl.loop(1, n)
    def _(step):
        og_arrival(step).wait_recv()
        act_arrival(wide_peer(step)).wait_recv()

    @pl.loop(0, 2)
    def _(half):
        for b in range(2):
            pencil = acts_in[:, half, b].reshape(4 * ch, cols)
            v = dot_nn(bigw[...], pencil)
            g = sigmoid_of(v)
            cot = og_in[:, half, b].reshape(4 * ch, cols).astype(F32)
            grad = (cot * (g * (1.0 + v * (1.0 - g)))).astype(BF16)
            dg[half, b] = grad
            back = dot_nn(bigw_t[...], grad).astype(BF16)
            ag_out[:, half, b] = back.reshape(4, ch, cols)
        for q in range(4):
            peer = 2 * q + half

            @pl.when(peer != me)
            def _():
                ag_copy(peer).start()

            @pl.when(peer == me)
            def _():
                ag_in[me] = ag_out[q, half]

    depth_acc[...] = jnp.zeros_like(depth_acc)
    plane_acc[...] = jnp.zeros_like(plane_acc)

    @pl.loop(0, 2)
    def _(half):
        for b in range(2):
            depth_acc[...] += dot_nt(dg[half, b], acts_in[:, half, b].reshape(4 * ch, cols))

    def diagonal(d):
        tile = jnp.zeros((ch, 128), F32)
        for q in range(4):
            for t in range(2):
                if 2 * t - q == d:
                    tile = tile + depth_acc[q * ch : (q + 1) * ch, 128 * t : 128 * (t + 1)]
        return tile

    in_low = lax.broadcasted_iota(jnp.int32, (ch, 128), 1) < ch
    for t in range(4):
        crossed = jnp.where(in_low, diagonal(2 * t - 2), diagonal(2 * t - 4))
        tile = diagonal(2 * t - 3) + pltpu.roll(crossed, 64, 1)
        red_f[:, 8 * t : 8 * (t + 1)] = tile.reshape(n, ch // n, 128)
    zr_src[...] = red_f[:, 0:DEPTH_ROWS].astype(BF16)

    @pl.loop(1, n)
    def _(step):
        z1_copy(wide_peer(step)).start()

    zr_in[me] = zr_src[me]

    @pl.loop(0, rows)
    def _(step):
        x = lax.rem(step + rows - 1, rows)

        @pl.when(x != me)
        def _():
            ag_arrival(x).wait_recv()

        for z in range(2):
            row = ag_in[x, z].astype(F32) * slope[x, z]
            shifted = shifted_stack(row.astype(BF16))
            stack[x + 1, z] = shifted
            plane_acc[...] += dot_nt(shifted, volh[pl.ds(x, 3), z].reshape(3 * ch, cols))

        @pl.when(step == 1)
        def _():
            @pl.when(has_high)
            def _():
                pg_up().start()

            @pl.when(has_low)
            def _():
                pg_down().start()

    for s in range(3):
        first = plane_acc[s * ch : (s + 1) * ch, 0:128]
        rest = jnp.concatenate(
            [plane_acc[s * ch : (s + 1) * ch, 128:192], jnp.zeros((ch, 64), F32)], axis=1
        )
        low = DEPTH_ROWS + 16 * s
        red_f[:, low : low + 8] = first.reshape(n, ch // n, 128)
        red_f[:, low + 8 : low + 16] = rest.reshape(n, ch // n, 128)
    red_src[...] = red_f[:, DEPTH_ROWS:ALL_ROWS].astype(BF16)

    @pl.loop(1, n)
    def _(step):
        r1_copy(wide_peer(step)).start()

    red_in[me] = red_src[me]

    def volume_rows(low, high):
        @pl.loop(low, high)
        def _(x):
            for z in range(2):
                out = dot_nn(wb[...], stack[pl.ds(x, 3), z].reshape(9 * ch, cols))
                vg[x, z] = (og[x, z].astype(F32) + out).astype(BF16)

    volume_rows(1, 3)

    @pl.loop(1, n)
    def _(step):
        z1_arrival(wide_peer(step)).wait_recv()
        r1_arrival(wide_peer(step)).wait_recv()

    part[0:DEPTH_ROWS] = jnp.sum(zr_in[...].astype(F32), axis=0).astype(BF16)
    part[DEPTH_ROWS:ALL_ROWS] = jnp.sum(red_in[...].astype(F32), axis=0).astype(BF16)

    @pl.loop(1, m)
    def _(step):
        r2_copy(narrow_peer(step)).start()

    part_in[mine] = part[...]
    volume_rows(3, 5)

    @pl.loop(1, m)
    def _(step):
        r2_arrival(narrow_peer(step)).wait_recv()

    tot[...] = (jnp.sum(part_in[...].astype(F32), axis=0) * scale).astype(BF16)

    @pl.loop(1, n)
    def _(step):
        r3_copy(wide_peer(step)).start()

    tot_in[me] = tot[...]
    volume_rows(5, rows - 1)

    @pl.when(has_high)
    def _():
        pg_up().wait_send()
        pg_down().wait_recv()

    @pl.when(has_low)
    def _():
        pg_down().wait_send()
        pg_up().wait_recv()

    @pl.when(has_low)
    def _():
        for z in range(2):
            stack[0, z] = shifted_stack(pg_halo[0, z])

    @pl.when(has_high)
    def _():
        for z in range(2):
            stack[rows + 1, z] = shifted_stack(pg_halo[1, z])

    @pl.when(jnp.logical_not(has_low))
    def _():
        stack[0] = jnp.zeros(stack.shape[1:], BF16)

    @pl.when(jnp.logical_not(has_high))
    def _():
        stack[rows + 1] = jnp.zeros(stack.shape[1:], BF16)

    volume_rows(0, 1)
    volume_rows(rows - 1, rows)

    @pl.loop(1, n)
    def _(step):
        peer = wide_peer(step)
        r3_arrival(peer).wait_recv()
        og_copy(step).wait_send()
        act_copy(peer).wait_send()
        ag_copy(peer).wait_send()
        z1_copy(peer).wait_send()
        r1_copy(peer).wait_send()
        r3_copy(peer).wait_send()

    @pl.loop(1, m)
    def _(step):
        r2_copy(narrow_peer(step)).wait_send()

    red_f[...] = tot_in[...].astype(F32)
    for t in range(4):
        tile = red_f[:, 8 * t : 8 * (t + 1)].reshape(ch, 128)
        depth_out[2 * t] = tile[:, 0:64]
        if t < 3:
            depth_out[2 * t + 1] = tile[:, 64:128]
    for s in range(3):
        low = DEPTH_ROWS + 16 * s
        first = red_f[:, low : low + 8].reshape(ch, 128)
        plane_out[2 - s] = first[:, 0:64]
        plane_out[5 - s] = first[:, 64:128]
        plane_out[8 - s] = red_f[:, low + 8 : low + 16].reshape(ch, 128)[:, 0:64]


def fused_block(n, m, volume, out_grad, plane_kernel, z_axis_kernel):
    ch, _, rows, cols = volume.shape
    vol = volume.transpose(2, 1, 0, 3)
    og = out_grad.transpose(2, 1, 0, 3)
    scale = 1.0 / math.sqrt(2 * n * rows * m * cols)
    own = (rows, 2, ch, cols)
    pencil = (4, 2, 2, ch, cols)
    sems = []
    for count in (2, n, n, n, 2, n, n, m, n):
        sems += [pltpu.SemaphoreType.DMA((count,))] * 2
    vmem = pl.BlockSpec(memory_space=pltpu.VMEM)
    vg, plane, depth = pl.pallas_call(
        functools.partial(block_kernel, n, m, rows, scale),
        out_shape=(
            jax.ShapeDtypeStruct(own, BF16),
            jax.ShapeDtypeStruct((9, ch, ch), F32),
            jax.ShapeDtypeStruct((7, ch, ch), F32),
        ),
        in_specs=[vmem] * 4,
        out_specs=(vmem, vmem, vmem),
        scratch_shapes=[
            pltpu.VMEM((ch, 9 * ch), BF16),
            pltpu.VMEM((ch, 9 * ch), BF16),
            pltpu.VMEM((4 * ch, 4 * ch), BF16),
            pltpu.VMEM((4 * ch, 4 * ch), BF16),
            pltpu.VMEM((rows + 2, 2, ch, cols), BF16),
            pltpu.VMEM((rows + 2, 2, 3 * ch, cols), BF16),
            pltpu.VMEM(own, F32),
            pltpu.VMEM(own, BF16),
            pltpu.VMEM(pencil, BF16),
            pltpu.VMEM(pencil, BF16),
            pltpu.VMEM((2, 2, 4 * ch, cols), BF16),
            pltpu.VMEM(pencil, BF16),
            pltpu.VMEM((n, 2, ch, cols), BF16),
            pltpu.VMEM((2, 2, ch, cols), BF16),
            pltpu.VMEM((3 * ch, 3 * ch), F32),
            pltpu.VMEM((4 * ch, 4 * ch), F32),
            pltpu.VMEM((n, ALL_ROWS, 128), F32),
            pltpu.VMEM((n, DEPTH_ROWS, 128), BF16),
            pltpu.VMEM((n, DEPTH_ROWS, 128), BF16),
            pltpu.VMEM((n, PLANE_ROWS, 128), BF16),
            pltpu.VMEM((n, PLANE_ROWS, 128), BF16),
            pltpu.VMEM((ALL_ROWS, 128), BF16),
            pltpu.VMEM((m, ALL_ROWS, 128), BF16),
            pltpu.VMEM((ALL_ROWS, 128), BF16),
            pltpu.VMEM((n, ALL_ROWS, 128), BF16),
        ]
        + sems,
        compiler_params=pltpu.CompilerParams(
            collective_id=0, has_side_effects=True, vmem_limit_bytes=52 * 1024 * 1024
        ),
    )(vol, og, plane_kernel, z_axis_kernel)
    return vg.transpose(2, 1, 0, 3), plane, depth


def solution(mesh):
    n, m = mesh.shape["wide"], mesh.shape["narrow"]

    def body(volume, out_grad, plane_kernel, z_axis_kernel):
        ch, slabs, rows, cols = volume.shape
        if n == 8 and slabs == 2 and rows == n and ch == 64 and m > 1:
            return fused_block(n, m, volume, out_grad, plane_kernel, z_axis_kernel)
        return on_device(volume, out_grad, plane_kernel, z_axis_kernel)

    return jax.shard_map(
        body,
        mesh=mesh,
        in_specs=(P(None, "wide", "narrow", None), P(None, "wide", "narrow", None), P(), P()),
        out_specs=(P(None, "wide", "narrow", None), P(), P()),
        check_vma=False,
    )
```

```python
import functools
import math

import jax
import jax.numpy as jnp
from jax import lax
from jax.experimental import pallas as pl
from jax.experimental.pallas import tpu as pltpu
from jax.sharding import PartitionSpec as P

Z_DILATION = 4


def with_halo(block, sides, width):
    for axis, dim in sides:
        count = lax.axis_size(axis)
        forward = [(i, i + 1) for i in range(count - 1)]
        backward = [(target, source) for source, target in forward]
        low = lax.ppermute(
            lax.slice_in_dim(block, block.shape[dim] - width, None, axis=dim), axis, forward
        )
        high = lax.ppermute(lax.slice_in_dim(block, 0, width, axis=dim), axis, backward)
        block = jnp.concatenate([low, block, high], axis=dim)
    return block


def silu_slope(values):
    sigmoid = jax.nn.sigmoid(values)
    return sigmoid * (1.0 + values * (1.0 - sigmoid))


def plane_stack(rimmed, rows, cols, flipped):
    padded = jnp.pad(rimmed, ((0, 0), (0, 0), (0, 0), (1, 1)))
    pieces = []
    for kernel_tap_index in range(9):
        source_tap = 8 - kernel_tap_index if flipped else kernel_tap_index
        row_shift = source_tap // 3
        col_shift = source_tap % 3
        pieces.append(padded[:, :, row_shift : row_shift + rows, col_shift : col_shift + cols])
    return jnp.concatenate(pieces, axis=0)


def depth_stack(pencil, kernel_extent, flipped):
    depth_axis_size = pencil.shape[1]
    padded = jnp.pad(pencil, ((0, 0), (kernel_extent, kernel_extent), (0, 0)))
    pieces = []
    for kernel_tap_index in range(7):
        source_tap = 6 - kernel_tap_index if flipped else kernel_tap_index
        start = source_tap * Z_DILATION
        pieces.append(padded[:, start : start + depth_axis_size])
    return jnp.concatenate(pieces, axis=0)


def stacked_mixing(weight, stacked, out_shape):
    mixed = jnp.dot(
        weight, stacked.reshape(stacked.shape[0], -1), preferred_element_type=jnp.float32
    )
    return mixed.reshape(out_shape)


def stacked_kernel_grad(left, stacked, taps):
    width = left.shape[0]
    product = jnp.dot(
        left.reshape(width, -1),
        stacked.reshape(stacked.shape[0], -1).T,
        preferred_element_type=jnp.float32,
    )
    return product.reshape(width, taps, width).transpose(1, 0, 2)


def on_device(volume, out_grad, plane_kernel, z_axis_kernel):
    width, slabs, rows, cols = volume.shape
    cells = rows * cols
    kernel_extent = 3 * Z_DILATION
    plane_forward = plane_kernel.transpose(1, 0, 2).reshape(width, 9 * width)
    plane_backward = plane_kernel.transpose(2, 0, 1).reshape(width, 9 * width)
    depth_forward = z_axis_kernel.transpose(1, 0, 2).reshape(width, 7 * width)
    depth_backward = z_axis_kernel.transpose(2, 0, 1).reshape(width, 7 * width)
    rimmed = with_halo(volume, (("narrow", 2),), 1)
    volume_stack = plane_stack(rimmed, rows, cols, False)
    pre_act = stacked_mixing(plane_forward, volume_stack, volume.shape)
    acts = jax.nn.silu(pre_act).astype(jnp.bfloat16)
    act_slab = acts.reshape(width, slabs, cells)
    act_pencil, grad_pencil = (
        lax.all_to_all(act_slab, "wide", split_axis=2, concat_axis=1, tiled=True),
        lax.all_to_all(
            out_grad.reshape(width, slabs, cells), "wide", split_axis=2, concat_axis=1, tiled=True
        ),
    )
    depth_axis_size = act_pencil.shape[1]
    act_stack = depth_stack(act_pencil, kernel_extent, False)
    depth_output = stacked_mixing(depth_forward, act_stack, act_pencil.shape)
    depth_gradient = (grad_pencil.astype(jnp.float32) * silu_slope(depth_output)).astype(
        jnp.bfloat16
    )
    depth_term = stacked_kernel_grad(depth_gradient, act_stack, 7)
    grad_stack = depth_stack(depth_gradient, kernel_extent, True)
    activation_gradient = stacked_mixing(depth_backward, grad_stack, act_pencil.shape).astype(
        jnp.bfloat16
    )
    slab_grad = lax.all_to_all(
        activation_gradient, "wide", split_axis=1, concat_axis=2, tiled=True
    ).reshape(width, slabs, rows, cols)
    gradient_scale = 1.0 / math.sqrt(depth_axis_size * rows * lax.axis_size("narrow") * cols)
    pre_grad = (slab_grad.astype(jnp.float32) * silu_slope(pre_act)).astype(jnp.bfloat16)
    plane_term = stacked_kernel_grad(pre_grad, volume_stack, 9)
    grad_rimmed = with_halo(pre_grad, (("narrow", 2),), 1)
    pre_stack = plane_stack(grad_rimmed, rows, cols, True)
    volume_grad = out_grad.astype(jnp.float32) + stacked_mixing(
        plane_backward, pre_stack, volume.shape
    )
    plane_total, depth_total = lax.psum((plane_term, depth_term), ("wide", "narrow"))
    return (
        volume_grad.astype(jnp.bfloat16),
        plane_total * gradient_scale,
        depth_total * gradient_scale,
    )


BF16 = jnp.bfloat16
F32 = jnp.float32
MESH = pl.DeviceIdType.MESH
DEPTH_ROWS = 32
PLANE_ROWS = 48
ALL_ROWS = 80


def sigmoid_of(values):
    return 0.5 * jnp.tanh(0.5 * values) + 0.5


def shifted_stack(row):
    wide_row = row.astype(F32)
    cols = row.shape[1]
    column = lax.broadcasted_iota(jnp.int32, row.shape, 1)
    left = jnp.where(column == 0, 0.0, pltpu.roll(wide_row, 1, 1))
    right = jnp.where(column == cols - 1, 0.0, pltpu.roll(wide_row, cols - 1, 1))
    return jnp.concatenate([left.astype(BF16), row.astype(BF16), right.astype(BF16)], axis=0)


def dot_nn(left, right):
    return jnp.dot(left, right, preferred_element_type=F32)


def dot_nt(left, right):
    return lax.dot_general(left, right, (((1,), (1,)), ((), ())), preferred_element_type=F32)


def block_kernel(
    n, m, rows, scale,
    vol, og, plane_w, depth_w,
    vg, plane_out, depth_out,
    wf, wb, bigw, bigw_t,
    volh, stack, slope, acts_out, acts_in, og_in, dg, ag_out, ag_in, pg_halo, plane_acc, depth_acc,
    red_f, zr_src, zr_in, red_src, red_in, part, part_in, tot, tot_in,
    vh_s, vh_r, og_s, og_r, ac_s, ac_r, ag_s, ag_r, ph_s, ph_r, z1_s, z1_r, r1_s, r1_r, r2_s, r2_r, r3_s, r3_r,
):
    me = lax.axis_index("wide")
    mine = lax.axis_index("narrow")
    ch = vol.shape[2]
    cols = vol.shape[3]

    def rcopy(source, target, send, recv, **where):
        return pltpu.make_async_remote_copy(
            src_ref=source, dst_ref=target, send_sem=send, recv_sem=recv,
            device_id=where, device_id_type=MESH,
        )

    def wide_peer(step):
        return lax.rem(me + step, n)

    def narrow_peer(step):
        return lax.rem(mine + step, m)

    barrier = pltpu.get_barrier_semaphore()

    @pl.loop(1, n)
    def _(step):
        pl.semaphore_signal(barrier, inc=1, device_id={"wide": wide_peer(step)}, device_id_type=MESH)

    @pl.loop(1, m)
    def _(step):
        pl.semaphore_signal(barrier, inc=1, device_id={"narrow": narrow_peer(step)}, device_id_type=MESH)

    for t in range(4):
        wf[:, 128 * t : 128 * (t + 1)] = jnp.concatenate([plane_w[2 * t], plane_w[2 * t + 1]], axis=1)
        pair = jnp.concatenate([plane_w[8 - 2 * t], plane_w[7 - 2 * t]], axis=0)
        wb[:, 128 * t : 128 * (t + 1)] = pair.astype(F32).T.astype(BF16)
    wf[:, 512:576] = plane_w[8]
    wb[:, 512:576] = plane_w[0].astype(F32).T.astype(BF16)
    for q in range(4):
        band = jnp.concatenate([depth_w[3 - q + p] for p in range(4)], axis=1)
        bigw[q * ch : (q + 1) * ch] = band
        bigw_t[:, q * ch : (q + 1) * ch] = band.astype(F32).T.astype(BF16)

    pl.semaphore_wait(barrier, n + m - 2)

    has_low = mine > 0
    has_high = mine < m - 1
    up = jnp.minimum(mine + 1, m - 1)
    down = jnp.maximum(mine - 1, 0)

    def vol_up():
        return rcopy(vol.at[rows - 1], volh.at[0], vh_s.at[0], vh_r.at[0], narrow=up)

    def vol_down():
        return rcopy(vol.at[0], volh.at[rows + 1], vh_s.at[1], vh_r.at[1], narrow=down)

    def og_copy(peer, z):
        return rcopy(
            og.at[peer, z], og_in.at[me // 2, lax.rem(me, 2), z],
            og_s.at[n * z + peer], og_r.at[n * z + me], wide=peer,
        )

    def og_arrival(peer, z):
        return rcopy(
            og.at[peer, z], og_in.at[peer // 2, lax.rem(peer, 2), z],
            og_s.at[n * z + peer], og_r.at[n * z + peer], wide=peer,
        )

    def act_copy(peer, z):
        return rcopy(
            acts_out.at[peer, z], acts_in.at[me // 2, lax.rem(me, 2), z],
            ac_s.at[n * z + peer], ac_r.at[n * z + me], wide=peer,
        )

    def act_arrival(peer, z):
        return rcopy(
            acts_out.at[peer, z], acts_in.at[peer // 2, lax.rem(peer, 2), z],
            ac_s.at[n * z + peer], ac_r.at[n * z + peer], wide=peer,
        )

    def ag_copy(peer, z):
        return rcopy(
            ag_out.at[peer // 2, lax.rem(peer, 2), z], ag_in.at[me, z],
            ag_s.at[n * z + peer], ag_r.at[n * z + me], wide=peer,
        )

    def ag_arrival(peer, z):
        return rcopy(
            ag_out.at[peer // 2, lax.rem(peer, 2), z], ag_in.at[peer, z],
            ag_s.at[n * z + peer], ag_r.at[n * z + peer], wide=peer,
        )

    def pg_up(z):
        return rcopy(
            stack.at[rows, z, pl.ds(ch, ch)], pg_halo.at[0, z], ph_s.at[2 * z], ph_r.at[2 * z], narrow=up
        )

    def pg_down(z):
        return rcopy(
            stack.at[1, z, pl.ds(ch, ch)], pg_halo.at[1, z], ph_s.at[2 * z + 1], ph_r.at[2 * z + 1], narrow=down
        )

    def z1_copy(peer):
        return rcopy(zr_src.at[peer], zr_in.at[me], z1_s.at[peer], z1_r.at[me], wide=peer)

    def z1_arrival(peer):
        return rcopy(zr_src.at[peer], zr_in.at[peer], z1_s.at[peer], z1_r.at[peer], wide=peer)

    def r1_copy(peer):
        return rcopy(red_src.at[peer], red_in.at[me], r1_s.at[peer], r1_r.at[me], wide=peer)

    def r1_arrival(peer):
        return rcopy(red_src.at[peer], red_in.at[peer], r1_s.at[peer], r1_r.at[peer], wide=peer)

    def r2_copy(peer):
        return rcopy(part, part_in.at[mine], r2_s.at[peer], r2_r.at[mine], narrow=peer)

    def r2_arrival(peer):
        return rcopy(part, part_in.at[peer], r2_s.at[peer], r2_r.at[peer], narrow=peer)

    def r3_copy(peer):
        return rcopy(tot, tot_in.at[me], r3_s.at[peer], r3_r.at[me], wide=peer)

    def r3_arrival(peer):
        return rcopy(tot, tot_in.at[peer], r3_s.at[peer], r3_r.at[peer], wide=peer)

    @pl.when(has_high)
    def _():
        vol_up().start()

    @pl.when(has_low)
    def _():
        vol_down().start()

    @pl.loop(1, n)
    def _(step):
        og_copy(wide_peer(step), 0).start()

    og_in[me // 2, lax.rem(me, 2)] = og[me]

    @pl.when(jnp.logical_not(has_low))
    def _():
        volh[0] = jnp.zeros(volh.shape[1:], BF16)

    @pl.when(jnp.logical_not(has_high))
    def _():
        volh[rows + 1] = jnp.zeros(volh.shape[1:], BF16)

    def stack_rows(z):
        @pl.loop(0, rows)
        def _(x):
            row = vol[x, z]
            volh[x + 1, z] = row
            stack[x + 1, z] = shifted_stack(row)

    def forward_rows(z):
        for x in (0, rows + 1):
            stack[x, z] = shifted_stack(volh[x, z])

        @pl.loop(1, n + 1)
        def _(step):
            x = wide_peer(step)
            v = dot_nn(wf[...], stack[pl.ds(x, 3), z].reshape(9 * ch, cols))
            g = sigmoid_of(v)
            acts_out[x, z] = (v * g).astype(BF16)
            slope[x, z] = g * (1.0 + v * (1.0 - g))

            @pl.when(step < n)
            def _():
                act_copy(x, z).start()

        acts_in[me // 2, lax.rem(me, 2), z] = acts_out[me, z]

    stack_rows(0)

    @pl.when(has_high)
    def _():
        vol_up().wait_send()
        vol_down().wait_recv()

    @pl.when(has_low)
    def _():
        vol_down().wait_send()
        vol_up().wait_recv()

    forward_rows(0)

    @pl.loop(1, n)
    def _(step):
        og_copy(wide_peer(step), 1).start()

    stack_rows(1)
    forward_rows(1)
    depth_acc[...] = jnp.zeros_like(depth_acc)
    plane_acc[...] = jnp.zeros_like(plane_acc)

    for z in range(2):
        @pl.loop(1, n)
        def _(step):
            og_arrival(wide_peer(step), z).wait_recv()
            act_arrival(wide_peer(step), z).wait_recv()

        @pl.loop(0, 2)
        def _(half):
            pencil = acts_in[:, half, z].reshape(4 * ch, cols)
            v = dot_nn(bigw[...], pencil)
            g = sigmoid_of(v)
            cot = og_in[:, half, z].reshape(4 * ch, cols).astype(F32)
            grad = (cot * (g * (1.0 + v * (1.0 - g)))).astype(BF16)
            dg[half, z] = grad
            back = dot_nn(bigw_t[...], grad).astype(BF16)
            ag_out[:, half, z] = back.reshape(4, ch, cols)
            for q in range(4):
                peer = 2 * q + half

                @pl.when(peer != me)
                def _():
                    ag_copy(peer, z).start()

                @pl.when(peer == me)
                def _():
                    ag_in[me, z] = ag_out[q, half, z]

        @pl.loop(0, 2)
        def _(half):
            depth_acc[...] += dot_nt(dg[half, z], acts_in[:, half, z].reshape(4 * ch, cols))

    def diagonal(d):
        tile = jnp.zeros((ch, 128), F32)
        for q in range(4):
            for t in range(2):
                if 2 * t - q == d:
                    tile = tile + depth_acc[q * ch : (q + 1) * ch, 128 * t : 128 * (t + 1)]
        return tile

    in_low = lax.broadcasted_iota(jnp.int32, (ch, 128), 1) < ch
    for t in range(4):
        crossed = jnp.where(in_low, diagonal(2 * t - 2), diagonal(2 * t - 4))
        tile = diagonal(2 * t - 3) + pltpu.roll(crossed, 64, 1)
        red_f[:, 8 * t : 8 * (t + 1)] = tile.reshape(n, ch // n, 128)
    zr_src[...] = red_f[:, 0:DEPTH_ROWS].astype(BF16)

    @pl.loop(1, n)
    def _(step):
        z1_copy(wide_peer(step)).start()

    zr_in[me] = zr_src[me]

    def pre_rows(z):
        @pl.loop(0, rows)
        def _(step):
            x = lax.rem(step + rows - 1, rows)

            @pl.when(x != me)
            def _():
                ag_arrival(x, z).wait_recv()

            row = ag_in[x, z].astype(F32) * slope[x, z]
            shifted = shifted_stack(row.astype(BF16))
            stack[x + 1, z] = shifted
            plane_acc[...] += dot_nt(shifted, volh[pl.ds(x, 3), z].reshape(3 * ch, cols))

            @pl.when(step == 1)
            def _():
                @pl.when(has_high)
                def _():
                    pg_up(z).start()

                @pl.when(has_low)
                def _():
                    pg_down(z).start()

    def volume_rows(z, low, high):
        @pl.loop(low, high)
        def _(x):
            out = dot_nn(wb[...], stack[pl.ds(x, 3), z].reshape(9 * ch, cols))
            vg[x, z] = (og[x, z].astype(F32) + out).astype(BF16)

    def edge_rows(z):
        @pl.when(has_high)
        def _():
            pg_up(z).wait_send()
            pg_down(z).wait_recv()
            stack[rows + 1, z] = shifted_stack(pg_halo[1, z])

        @pl.when(has_low)
        def _():
            pg_down(z).wait_send()
            pg_up(z).wait_recv()
            stack[0, z] = shifted_stack(pg_halo[0, z])

        @pl.when(jnp.logical_not(has_low))
        def _():
            stack[0, z] = jnp.zeros(stack.shape[2:], BF16)

        @pl.when(jnp.logical_not(has_high))
        def _():
            stack[rows + 1, z] = jnp.zeros(stack.shape[2:], BF16)

        volume_rows(z, 0, 1)
        volume_rows(z, rows - 1, rows)

    pre_rows(0)
    volume_rows(0, 1, rows - 1)
    pre_rows(1)

    for s in range(3):
        first = plane_acc[s * ch : (s + 1) * ch, 0:128]
        rest = jnp.concatenate(
            [plane_acc[s * ch : (s + 1) * ch, 128:192], jnp.zeros((ch, 64), F32)], axis=1
        )
        low = DEPTH_ROWS + 16 * s
        red_f[:, low : low + 8] = first.reshape(n, ch // n, 128)
        red_f[:, low + 8 : low + 16] = rest.reshape(n, ch // n, 128)
    red_src[...] = red_f[:, DEPTH_ROWS:ALL_ROWS].astype(BF16)

    @pl.loop(1, n)
    def _(step):
        r1_copy(wide_peer(step)).start()

    red_in[me] = red_src[me]

    volume_rows(1, 1, 4)

    @pl.loop(1, n)
    def _(step):
        z1_arrival(wide_peer(step)).wait_recv()
        r1_arrival(wide_peer(step)).wait_recv()

    part[0:DEPTH_ROWS] = jnp.sum(zr_in[...].astype(F32), axis=0).astype(BF16)
    part[DEPTH_ROWS:ALL_ROWS] = jnp.sum(red_in[...].astype(F32), axis=0).astype(BF16)

    @pl.loop(1, m)
    def _(step):
        r2_copy(narrow_peer(step)).start()

    part_in[mine] = part[...]
    edge_rows(0)

    @pl.loop(1, m)
    def _(step):
        r2_arrival(narrow_peer(step)).wait_recv()

    tot[...] = (jnp.sum(part_in[...].astype(F32), axis=0) * scale).astype(BF16)

    @pl.loop(1, n)
    def _(step):
        r3_copy(wide_peer(step)).start()

    tot_in[me] = tot[...]
    volume_rows(1, 4, rows - 1)
    edge_rows(1)

    @pl.loop(1, n)
    def _(step):
        peer = wide_peer(step)
        r3_arrival(peer).wait_recv()
        for z in range(2):
            og_copy(peer, z).wait_send()
            act_copy(peer, z).wait_send()
            ag_copy(peer, z).wait_send()
        z1_copy(peer).wait_send()
        r1_copy(peer).wait_send()
        r3_copy(peer).wait_send()

    @pl.loop(1, m)
    def _(step):
        r2_copy(narrow_peer(step)).wait_send()

    red_f[...] = tot_in[...].astype(F32)
    for t in range(4):
        tile = red_f[:, 8 * t : 8 * (t + 1)].reshape(ch, 128)
        depth_out[2 * t] = tile[:, 0:64]
        if t < 3:
            depth_out[2 * t + 1] = tile[:, 64:128]
    for s in range(3):
        low = DEPTH_ROWS + 16 * s
        first = red_f[:, low : low + 8].reshape(ch, 128)
        plane_out[2 - s] = first[:, 0:64]
        plane_out[5 - s] = first[:, 64:128]
        plane_out[8 - s] = red_f[:, low + 8 : low + 16].reshape(ch, 128)[:, 0:64]


def fused_block(n, m, volume, out_grad, plane_kernel, z_axis_kernel):
    ch, _, rows, cols = volume.shape
    vol = volume.transpose(2, 1, 0, 3)
    og = out_grad.transpose(2, 1, 0, 3)
    scale = 1.0 / math.sqrt(2 * n * rows * m * cols)
    own = (rows, 2, ch, cols)
    pencil = (4, 2, 2, ch, cols)
    sems = []
    for count in (2, 2 * n, 2 * n, 2 * n, 4, n, n, m, n):
        sems += [pltpu.SemaphoreType.DMA((count,))] * 2
    vmem = pl.BlockSpec(memory_space=pltpu.VMEM)
    vg, plane, depth = pl.pallas_call(
        functools.partial(block_kernel, n, m, rows, scale),
        out_shape=(
            jax.ShapeDtypeStruct(own, BF16),
            jax.ShapeDtypeStruct((9, ch, ch), F32),
            jax.ShapeDtypeStruct((7, ch, ch), F32),
        ),
        in_specs=[vmem] * 4,
        out_specs=(vmem, vmem, vmem),
        scratch_shapes=[
            pltpu.VMEM((ch, 9 * ch), BF16),
            pltpu.VMEM((ch, 9 * ch), BF16),
            pltpu.VMEM((4 * ch, 4 * ch), BF16),
            pltpu.VMEM((4 * ch, 4 * ch), BF16),
            pltpu.VMEM((rows + 2, 2, ch, cols), BF16),
            pltpu.VMEM((rows + 2, 2, 3 * ch, cols), BF16),
            pltpu.VMEM(own, F32),
            pltpu.VMEM(own, BF16),
            pltpu.VMEM(pencil, BF16),
            pltpu.VMEM(pencil, BF16),
            pltpu.VMEM((2, 2, 4 * ch, cols), BF16),
            pltpu.VMEM(pencil, BF16),
            pltpu.VMEM((n, 2, ch, cols), BF16),
            pltpu.VMEM((2, 2, ch, cols), BF16),
            pltpu.VMEM((3 * ch, 3 * ch), F32),
            pltpu.VMEM((4 * ch, 4 * ch), F32),
            pltpu.VMEM((n, ALL_ROWS, 128), F32),
            pltpu.VMEM((n, DEPTH_ROWS, 128), BF16),
            pltpu.VMEM((n, DEPTH_ROWS, 128), BF16),
            pltpu.VMEM((n, PLANE_ROWS, 128), BF16),
            pltpu.VMEM((n, PLANE_ROWS, 128), BF16),
            pltpu.VMEM((ALL_ROWS, 128), BF16),
            pltpu.VMEM((m, ALL_ROWS, 128), BF16),
            pltpu.VMEM((ALL_ROWS, 128), BF16),
            pltpu.VMEM((n, ALL_ROWS, 128), BF16),
        ]
        + sems,
        compiler_params=pltpu.CompilerParams(
            collective_id=0, has_side_effects=True, vmem_limit_bytes=52 * 1024 * 1024
        ),
    )(vol, og, plane_kernel, z_axis_kernel)
    return vg.transpose(2, 1, 0, 3), plane, depth


def solution(mesh):
    n, m = mesh.shape["wide"], mesh.shape["narrow"]

    def body(volume, out_grad, plane_kernel, z_axis_kernel):
        ch, slabs, rows, cols = volume.shape
        if n == 8 and slabs == 2 and rows == n and ch == 64 and m > 1:
            return fused_block(n, m, volume, out_grad, plane_kernel, z_axis_kernel)
        return on_device(volume, out_grad, plane_kernel, z_axis_kernel)

    return jax.shard_map(
        body,
        mesh=mesh,
        in_specs=(P(None, "wide", "narrow", None), P(None, "wide", "narrow", None), P(), P()),
        out_specs=(P(None, "wide", "narrow", None), P(), P()),
        check_vma=False,
    )
```

```python
import functools
import math

import jax
import jax.numpy as jnp
from jax import lax
from jax.experimental import pallas as pl
from jax.experimental.pallas import tpu as pltpu
from jax.sharding import PartitionSpec as P

Z_DILATION = 4


def with_halo(block, sides, width):
    for axis, dim in sides:
        count = lax.axis_size(axis)
        forward = [(i, i + 1) for i in range(count - 1)]
        backward = [(target, source) for source, target in forward]
        low = lax.ppermute(
            lax.slice_in_dim(block, block.shape[dim] - width, None, axis=dim), axis, forward
        )
        high = lax.ppermute(lax.slice_in_dim(block, 0, width, axis=dim), axis, backward)
        block = jnp.concatenate([low, block, high], axis=dim)
    return block


def silu_slope(values):
    sigmoid = jax.nn.sigmoid(values)
    return sigmoid * (1.0 + values * (1.0 - sigmoid))


def plane_stack(rimmed, rows, cols, flipped):
    padded = jnp.pad(rimmed, ((0, 0), (0, 0), (0, 0), (1, 1)))
    pieces = []
    for kernel_tap_index in range(9):
        source_tap = 8 - kernel_tap_index if flipped else kernel_tap_index
        row_shift = source_tap // 3
        col_shift = source_tap % 3
        pieces.append(padded[:, :, row_shift : row_shift + rows, col_shift : col_shift + cols])
    return jnp.concatenate(pieces, axis=0)


def depth_stack(pencil, kernel_extent, flipped):
    depth_axis_size = pencil.shape[1]
    padded = jnp.pad(pencil, ((0, 0), (kernel_extent, kernel_extent), (0, 0)))
    pieces = []
    for kernel_tap_index in range(7):
        source_tap = 6 - kernel_tap_index if flipped else kernel_tap_index
        start = source_tap * Z_DILATION
        pieces.append(padded[:, start : start + depth_axis_size])
    return jnp.concatenate(pieces, axis=0)


def stacked_mixing(weight, stacked, out_shape):
    mixed = jnp.dot(
        weight, stacked.reshape(stacked.shape[0], -1), preferred_element_type=jnp.float32
    )
    return mixed.reshape(out_shape)


def stacked_kernel_grad(left, stacked, taps):
    width = left.shape[0]
    product = jnp.dot(
        left.reshape(width, -1),
        stacked.reshape(stacked.shape[0], -1).T,
        preferred_element_type=jnp.float32,
    )
    return product.reshape(width, taps, width).transpose(1, 0, 2)


def on_device(volume, out_grad, plane_kernel, z_axis_kernel):
    width, slabs, rows, cols = volume.shape
    cells = rows * cols
    kernel_extent = 3 * Z_DILATION
    plane_forward = plane_kernel.transpose(1, 0, 2).reshape(width, 9 * width)
    plane_backward = plane_kernel.transpose(2, 0, 1).reshape(width, 9 * width)
    depth_forward = z_axis_kernel.transpose(1, 0, 2).reshape(width, 7 * width)
    depth_backward = z_axis_kernel.transpose(2, 0, 1).reshape(width, 7 * width)
    rimmed = with_halo(volume, (("narrow", 2),), 1)
    volume_stack = plane_stack(rimmed, rows, cols, False)
    pre_act = stacked_mixing(plane_forward, volume_stack, volume.shape)
    acts = jax.nn.silu(pre_act).astype(jnp.bfloat16)
    act_slab = acts.reshape(width, slabs, cells)
    act_pencil, grad_pencil = (
        lax.all_to_all(act_slab, "wide", split_axis=2, concat_axis=1, tiled=True),
        lax.all_to_all(
            out_grad.reshape(width, slabs, cells), "wide", split_axis=2, concat_axis=1, tiled=True
        ),
    )
    depth_axis_size = act_pencil.shape[1]
    act_stack = depth_stack(act_pencil, kernel_extent, False)
    depth_output = stacked_mixing(depth_forward, act_stack, act_pencil.shape)
    depth_gradient = (grad_pencil.astype(jnp.float32) * silu_slope(depth_output)).astype(
        jnp.bfloat16
    )
    depth_term = stacked_kernel_grad(depth_gradient, act_stack, 7)
    grad_stack = depth_stack(depth_gradient, kernel_extent, True)
    activation_gradient = stacked_mixing(depth_backward, grad_stack, act_pencil.shape).astype(
        jnp.bfloat16
    )
    slab_grad = lax.all_to_all(
        activation_gradient, "wide", split_axis=1, concat_axis=2, tiled=True
    ).reshape(width, slabs, rows, cols)
    gradient_scale = 1.0 / math.sqrt(depth_axis_size * rows * lax.axis_size("narrow") * cols)
    pre_grad = (slab_grad.astype(jnp.float32) * silu_slope(pre_act)).astype(jnp.bfloat16)
    plane_term = stacked_kernel_grad(pre_grad, volume_stack, 9)
    grad_rimmed = with_halo(pre_grad, (("narrow", 2),), 1)
    pre_stack = plane_stack(grad_rimmed, rows, cols, True)
    volume_grad = out_grad.astype(jnp.float32) + stacked_mixing(
        plane_backward, pre_stack, volume.shape
    )
    plane_total, depth_total = lax.psum((plane_term, depth_term), ("wide", "narrow"))
    return (
        volume_grad.astype(jnp.bfloat16),
        plane_total * gradient_scale,
        depth_total * gradient_scale,
    )


BF16 = jnp.bfloat16
F32 = jnp.float32
MESH = pl.DeviceIdType.MESH
DEPTH_ROWS = 32
PLANE_ROWS = 48
ALL_ROWS = 80


def sigmoid_of(values):
    return 0.5 * jnp.tanh(0.5 * values) + 0.5


def shifted_stack(row):
    wide_row = row.astype(F32)
    cols = row.shape[1]
    column = lax.broadcasted_iota(jnp.int32, row.shape, 1)
    left = jnp.where(column == 0, 0.0, pltpu.roll(wide_row, 1, 1))
    right = jnp.where(column == cols - 1, 0.0, pltpu.roll(wide_row, cols - 1, 1))
    return jnp.concatenate([left.astype(BF16), row.astype(BF16), right.astype(BF16)], axis=0)


def dot_nn(left, right):
    return jnp.dot(left, right, preferred_element_type=F32)


def dot_nt(left, right):
    return lax.dot_general(left, right, (((1,), (1,)), ((), ())), preferred_element_type=F32)


def block_kernel(
    n, m, rows, scale,
    vol, og, plane_w, depth_w,
    vg, kernel_out,
    wf, wb, bigw, bigw_t,
    volh, stack, slope, acts_out, acts_in, og_in, dg, ag_out, ag_in, pg_halo, plane_acc, depth_acc,
    red_f, zr_src, zr_in, red_src, red_in, part, part_in, tot, tot_in,
    vh_s, vh_r, og_s, og_r, ac_s, ac_r, ag_s, ag_r, ph_s, ph_r, z1_s, z1_r, r1_s, r1_r, r2_s, r2_r, r3_s, r3_r,
):
    me = lax.axis_index("wide")
    mine = lax.axis_index("narrow")
    ch = vol.shape[2]
    cols = vol.shape[3]

    def rcopy(source, target, send, recv, **where):
        return pltpu.make_async_remote_copy(
            src_ref=source, dst_ref=target, send_sem=send, recv_sem=recv,
            device_id=where, device_id_type=MESH,
        )

    def wide_peer(step):
        spot = lax.rem(step * 3, 4)
        first, second, third = lax.rem(spot, 2), lax.rem(spot // 2, 2), lax.rem(step // 4, 2)
        core = lax.rem(me, 2)
        dx = first * (1 - core) + second * core
        dy = second * (1 - core) + first * core
        x = lax.rem(lax.rem(me // 2, 2) + dx, 2)
        y = lax.rem(me // 4 + dy, 2)
        return 4 * y + 2 * x + lax.rem(core + third, 2)

    def narrow_peer(step):
        return lax.rem(mine + step, m)

    barrier = pltpu.get_barrier_semaphore()

    @pl.loop(1, n)
    def _(step):
        pl.semaphore_signal(barrier, inc=1, device_id={"wide": wide_peer(step)}, device_id_type=MESH)

    @pl.loop(1, m)
    def _(step):
        pl.semaphore_signal(barrier, inc=1, device_id={"narrow": narrow_peer(step)}, device_id_type=MESH)

    for t in range(4):
        wf[:, 128 * t : 128 * (t + 1)] = jnp.concatenate([plane_w[2 * t], plane_w[2 * t + 1]], axis=1)
        pair = jnp.concatenate([plane_w[8 - 2 * t], plane_w[7 - 2 * t]], axis=0)
        wb[:, 128 * t : 128 * (t + 1)] = pair.astype(F32).T.astype(BF16)
    wf[:, 512:576] = plane_w[8]
    wb[:, 512:576] = plane_w[0].astype(F32).T.astype(BF16)
    for q in range(4):
        band = jnp.concatenate([depth_w[3 - q + p] for p in range(4)], axis=1)
        bigw[q * ch : (q + 1) * ch] = band
        bigw_t[:, q * ch : (q + 1) * ch] = band.astype(F32).T.astype(BF16)

    pl.semaphore_wait(barrier, n + m - 2)

    has_low = mine > 0
    has_high = mine < m - 1
    up = jnp.minimum(mine + 1, m - 1)
    down = jnp.maximum(mine - 1, 0)

    def vol_up():
        return rcopy(vol.at[rows - 1], volh.at[0], vh_s.at[0], vh_r.at[0], narrow=up)

    def vol_down():
        return rcopy(vol.at[0], volh.at[rows + 1], vh_s.at[1], vh_r.at[1], narrow=down)

    def og_copy(peer, z):
        return rcopy(
            og.at[peer, z], og_in.at[me // 2, lax.rem(me, 2), z],
            og_s.at[n * z + peer], og_r.at[n * z + me], wide=peer,
        )

    def og_arrival(peer, z):
        return rcopy(
            og.at[peer, z], og_in.at[peer // 2, lax.rem(peer, 2), z],
            og_s.at[n * z + peer], og_r.at[n * z + peer], wide=peer,
        )

    def act_copy(peer, z):
        return rcopy(
            acts_out.at[peer, z], acts_in.at[me // 2, lax.rem(me, 2), z],
            ac_s.at[n * z + peer], ac_r.at[n * z + me], wide=peer,
        )

    def act_arrival(peer, z):
        return rcopy(
            acts_out.at[peer, z], acts_in.at[peer // 2, lax.rem(peer, 2), z],
            ac_s.at[n * z + peer], ac_r.at[n * z + peer], wide=peer,
        )

    def ag_copy(peer, z):
        return rcopy(
            ag_out.at[peer // 2, lax.rem(peer, 2), z], ag_in.at[me, z],
            ag_s.at[n * z + peer], ag_r.at[n * z + me], wide=peer,
        )

    def ag_arrival(peer, z):
        return rcopy(
            ag_out.at[peer // 2, lax.rem(peer, 2), z], ag_in.at[peer, z],
            ag_s.at[n * z + peer], ag_r.at[n * z + peer], wide=peer,
        )

    def pg_up(z):
        return rcopy(
            stack.at[rows, z, pl.ds(ch, ch)], pg_halo.at[0, z], ph_s.at[2 * z], ph_r.at[2 * z], narrow=up
        )

    def pg_down(z):
        return rcopy(
            stack.at[1, z, pl.ds(ch, ch)], pg_halo.at[1, z], ph_s.at[2 * z + 1], ph_r.at[2 * z + 1], narrow=down
        )

    def z1_copy(peer):
        return rcopy(zr_src.at[peer], zr_in.at[me], z1_s.at[peer], z1_r.at[me], wide=peer)

    def z1_arrival(peer):
        return rcopy(zr_src.at[peer], zr_in.at[peer], z1_s.at[peer], z1_r.at[peer], wide=peer)

    def r1_copy(peer):
        return rcopy(red_src.at[peer], red_in.at[me], r1_s.at[peer], r1_r.at[me], wide=peer)

    def r1_arrival(peer):
        return rcopy(red_src.at[peer], red_in.at[peer], r1_s.at[peer], r1_r.at[peer], wide=peer)

    def r2_copy(peer):
        return rcopy(part, part_in.at[mine], r2_s.at[peer], r2_r.at[mine], narrow=peer)

    def r2_arrival(peer):
        return rcopy(part, part_in.at[peer], r2_s.at[peer], r2_r.at[peer], narrow=peer)

    def r3_copy(peer):
        return rcopy(tot, tot_in.at[me], r3_s.at[peer], r3_r.at[me], wide=peer)

    def r3_arrival(peer):
        return rcopy(tot, tot_in.at[peer], r3_s.at[peer], r3_r.at[peer], wide=peer)

    @pl.when(has_high)
    def _():
        vol_up().start()

    @pl.when(has_low)
    def _():
        vol_down().start()

    @pl.loop(1, n)
    def _(step):
        og_copy(wide_peer(step), 0).start()

    og_in[me // 2, lax.rem(me, 2)] = og[me]

    @pl.when(jnp.logical_not(has_low))
    def _():
        volh[0] = jnp.zeros(volh.shape[1:], BF16)

    @pl.when(jnp.logical_not(has_high))
    def _():
        volh[rows + 1] = jnp.zeros(volh.shape[1:], BF16)

    def stack_rows(z):
        @pl.loop(0, rows)
        def _(x):
            row = vol[x, z]
            volh[x + 1, z] = row
            stack[x + 1, z] = shifted_stack(row)

    def forward_rows(z):
        for x in (0, rows + 1):
            stack[x, z] = shifted_stack(volh[x, z])

        @pl.loop(1, n + 1)
        def _(step):
            x = wide_peer(step)
            v = dot_nn(wf[...], stack[pl.ds(x, 3), z].reshape(9 * ch, cols))
            g = sigmoid_of(v)
            acts_out[x, z] = (v * g).astype(BF16)
            slope[x, z] = g * (1.0 + v * (1.0 - g))

            @pl.when(step < n)
            def _():
                act_copy(x, z).start()

        acts_in[me // 2, lax.rem(me, 2), z] = acts_out[me, z]

    stack_rows(0)

    @pl.when(has_high)
    def _():
        vol_up().wait_send()
        vol_down().wait_recv()

    @pl.when(has_low)
    def _():
        vol_down().wait_send()
        vol_up().wait_recv()

    forward_rows(0)

    @pl.loop(1, n)
    def _(step):
        og_copy(wide_peer(step), 1).start()

    stack_rows(1)
    forward_rows(1)
    depth_acc[...] = jnp.zeros_like(depth_acc)
    plane_acc[...] = jnp.zeros_like(plane_acc)

    for z in range(2):
        @pl.loop(1, n)
        def _(step):
            og_arrival(wide_peer(step), z).wait_recv()
            act_arrival(wide_peer(step), z).wait_recv()

        @pl.loop(0, 2)
        def _(half):
            pencil = acts_in[:, half, z].reshape(4 * ch, cols)
            v = dot_nn(bigw[...], pencil)
            g = sigmoid_of(v)
            cot = og_in[:, half, z].reshape(4 * ch, cols).astype(F32)
            grad = (cot * (g * (1.0 + v * (1.0 - g)))).astype(BF16)
            dg[half, z] = grad
            back = dot_nn(bigw_t[...], grad).astype(BF16)
            ag_out[:, half, z] = back.reshape(4, ch, cols)
            for q in range(4):
                peer = 2 * q + half

                @pl.when(peer != me)
                def _():
                    ag_copy(peer, z).start()

                @pl.when(peer == me)
                def _():
                    ag_in[me, z] = ag_out[q, half, z]

        @pl.loop(0, 2)
        def _(half):
            depth_acc[...] += dot_nt(dg[half, z], acts_in[:, half, z].reshape(4 * ch, cols))

    def diagonal(d):
        tile = jnp.zeros((ch, 128), F32)
        for q in range(4):
            for t in range(2):
                if 2 * t - q == d:
                    tile = tile + depth_acc[q * ch : (q + 1) * ch, 128 * t : 128 * (t + 1)]
        return tile

    in_low = lax.broadcasted_iota(jnp.int32, (ch, 128), 1) < ch
    for t in range(4):
        crossed = jnp.where(in_low, diagonal(2 * t - 2), diagonal(2 * t - 4))
        tile = diagonal(2 * t - 3) + pltpu.roll(crossed, 64, 1)
        red_f[:, 8 * t : 8 * (t + 1)] = tile.reshape(n, ch // n, 128)
    zr_src[...] = red_f[:, 0:DEPTH_ROWS].astype(BF16)

    @pl.loop(1, n)
    def _(step):
        z1_copy(wide_peer(step)).start()

    zr_in[me] = zr_src[me]

    def pre_rows(z):
        @pl.loop(0, rows)
        def _(step):
            x = lax.rem(step + rows - 1, rows)

            @pl.when(x != me)
            def _():
                ag_arrival(x, z).wait_recv()

            row = ag_in[x, z].astype(F32) * slope[x, z]
            shifted = shifted_stack(row.astype(BF16))
            stack[x + 1, z] = shifted
            plane_acc[...] += dot_nt(shifted, volh[pl.ds(x, 3), z].reshape(3 * ch, cols))

            @pl.when(step == 1)
            def _():
                @pl.when(has_high)
                def _():
                    pg_up(z).start()

                @pl.when(has_low)
                def _():
                    pg_down(z).start()

    def volume_rows(z, low, high):
        @pl.loop(low, high)
        def _(x):
            out = dot_nn(wb[...], stack[pl.ds(x, 3), z].reshape(9 * ch, cols))
            vg[x, z] = (og[x, z].astype(F32) + out).astype(BF16)

    def edge_rows(z):
        @pl.when(has_high)
        def _():
            pg_up(z).wait_send()
            pg_down(z).wait_recv()
            stack[rows + 1, z] = shifted_stack(pg_halo[1, z])

        @pl.when(has_low)
        def _():
            pg_down(z).wait_send()
            pg_up(z).wait_recv()
            stack[0, z] = shifted_stack(pg_halo[0, z])

        @pl.when(jnp.logical_not(has_low))
        def _():
            stack[0, z] = jnp.zeros(stack.shape[2:], BF16)

        @pl.when(jnp.logical_not(has_high))
        def _():
            stack[rows + 1, z] = jnp.zeros(stack.shape[2:], BF16)

        volume_rows(z, 0, 1)
        volume_rows(z, rows - 1, rows)

    pre_rows(0)
    volume_rows(0, 1, rows - 1)
    pre_rows(1)

    for s in range(3):
        first = plane_acc[s * ch : (s + 1) * ch, 0:128]
        rest = jnp.concatenate(
            [plane_acc[s * ch : (s + 1) * ch, 128:192], jnp.zeros((ch, 64), F32)], axis=1
        )
        low = DEPTH_ROWS + 16 * s
        red_f[:, low : low + 8] = first.reshape(n, ch // n, 128)
        red_f[:, low + 8 : low + 16] = rest.reshape(n, ch // n, 128)
    red_src[...] = red_f[:, DEPTH_ROWS:ALL_ROWS].astype(BF16)

    @pl.loop(1, n)
    def _(step):
        r1_copy(wide_peer(step)).start()

    red_in[me] = red_src[me]

    volume_rows(1, 1, 4)

    @pl.loop(1, n)
    def _(step):
        z1_arrival(wide_peer(step)).wait_recv()
        r1_arrival(wide_peer(step)).wait_recv()

    part[0:DEPTH_ROWS] = jnp.sum(zr_in[...].astype(F32), axis=0).astype(BF16)
    part[DEPTH_ROWS:ALL_ROWS] = jnp.sum(red_in[...].astype(F32), axis=0).astype(BF16)

    @pl.loop(1, m)
    def _(step):
        r2_copy(narrow_peer(step)).start()

    part_in[mine] = part[...]
    edge_rows(0)

    @pl.loop(1, m)
    def _(step):
        r2_arrival(narrow_peer(step)).wait_recv()

    tot[...] = (jnp.sum(part_in[...].astype(F32), axis=0) * scale).astype(BF16)

    @pl.loop(1, n)
    def _(step):
        r3_copy(wide_peer(step)).start()

    tot_in[me] = tot[...]
    volume_rows(1, 4, rows - 1)
    edge_rows(1)

    @pl.loop(1, n)
    def _(step):
        peer = wide_peer(step)
        r3_arrival(peer).wait_recv()
        for z in range(2):
            og_copy(peer, z).wait_send()
            act_copy(peer, z).wait_send()
            ag_copy(peer, z).wait_send()
        z1_copy(peer).wait_send()
        r1_copy(peer).wait_send()
        r3_copy(peer).wait_send()

    @pl.loop(1, m)
    def _(step):
        r2_copy(narrow_peer(step)).wait_send()

    red_f[...] = tot_in[...].astype(F32)
    for t in range(4):
        tile = red_f[:, 8 * t : 8 * (t + 1)].reshape(ch, 128)
        kernel_out[9 + 2 * t] = tile[:, 0:64]
        if t < 3:
            kernel_out[10 + 2 * t] = tile[:, 64:128]
    for s in range(3):
        low = DEPTH_ROWS + 16 * s
        first = red_f[:, low : low + 8].reshape(ch, 128)
        kernel_out[2 - s] = first[:, 0:64]
        kernel_out[5 - s] = first[:, 64:128]
        kernel_out[8 - s] = red_f[:, low + 8 : low + 16].reshape(ch, 128)[:, 0:64]


def fused_block(n, m, volume, out_grad, plane_kernel, z_axis_kernel):
    ch, _, rows, cols = volume.shape
    vol = volume.transpose(2, 1, 0, 3)
    og = out_grad.transpose(2, 1, 0, 3)
    scale = 1.0 / math.sqrt(2 * n * rows * m * cols)
    own = (rows, 2, ch, cols)
    pencil = (4, 2, 2, ch, cols)
    sems = []
    for count in (2, 2 * n, 2 * n, 2 * n, 4, n, n, m, n):
        sems += [pltpu.SemaphoreType.DMA((count,))] * 2
    vmem = pl.BlockSpec(memory_space=pltpu.VMEM)
    vg, grads = pl.pallas_call(
        functools.partial(block_kernel, n, m, rows, scale),
        out_shape=(
            jax.ShapeDtypeStruct(own, BF16),
            jax.ShapeDtypeStruct((16, ch, ch), F32),
        ),
        in_specs=[vmem] * 4,
        out_specs=(vmem, vmem),
        scratch_shapes=[
            pltpu.VMEM((ch, 9 * ch), BF16),
            pltpu.VMEM((ch, 9 * ch), BF16),
            pltpu.VMEM((4 * ch, 4 * ch), BF16),
            pltpu.VMEM((4 * ch, 4 * ch), BF16),
            pltpu.VMEM((rows + 2, 2, ch, cols), BF16),
            pltpu.VMEM((rows + 2, 2, 3 * ch, cols), BF16),
            pltpu.VMEM(own, F32),
            pltpu.VMEM(own, BF16),
            pltpu.VMEM(pencil, BF16),
            pltpu.VMEM(pencil, BF16),
            pltpu.VMEM((2, 2, 4 * ch, cols), BF16),
            pltpu.VMEM(pencil, BF16),
            pltpu.VMEM((n, 2, ch, cols), BF16),
            pltpu.VMEM((2, 2, ch, cols), BF16),
            pltpu.VMEM((3 * ch, 3 * ch), F32),
            pltpu.VMEM((4 * ch, 4 * ch), F32),
            pltpu.VMEM((n, ALL_ROWS, 128), F32),
            pltpu.VMEM((n, DEPTH_ROWS, 128), BF16),
            pltpu.VMEM((n, DEPTH_ROWS, 128), BF16),
            pltpu.VMEM((n, PLANE_ROWS, 128), BF16),
            pltpu.VMEM((n, PLANE_ROWS, 128), BF16),
            pltpu.VMEM((ALL_ROWS, 128), BF16),
            pltpu.VMEM((m, ALL_ROWS, 128), BF16),
            pltpu.VMEM((ALL_ROWS, 128), BF16),
            pltpu.VMEM((n, ALL_ROWS, 128), BF16),
        ]
        + sems,
        compiler_params=pltpu.CompilerParams(
            collective_id=0, has_side_effects=True, vmem_limit_bytes=52 * 1024 * 1024
        ),
    )(vol, og, plane_kernel, z_axis_kernel)
    return vg.transpose(2, 1, 0, 3), grads[:9], grads[9:]


def solution(mesh):
    n, m = mesh.shape["wide"], mesh.shape["narrow"]

    def body(volume, out_grad, plane_kernel, z_axis_kernel):
        ch, slabs, rows, cols = volume.shape
        if n == 8 and slabs == 2 and rows == n and ch == 64 and m > 1:
            return fused_block(n, m, volume, out_grad, plane_kernel, z_axis_kernel)
        return on_device(volume, out_grad, plane_kernel, z_axis_kernel)

    return jax.shard_map(
        body,
        mesh=mesh,
        in_specs=(P(None, "wide", "narrow", None), P(None, "wide", "narrow", None), P(), P()),
        out_specs=(P(None, "wide", "narrow", None), P(), P()),
        check_vma=False,
    )
```
